32 devices in a mesh: grp: 2 (over x), ep: 16 (over z, y, core).
Axes of the slice: x: 2, y: 2, z: 4, core: 2. Of those that a mesh axis runs over, the one named last changes fastest.
Arguments:
- tokens: bfloat16 [2048, 2048], P(('grp', 'ep')), parts along dimension 0, may hold values from -6 to 6
- router_logits: float32 [2048, 8], P(('grp', 'ep')), parts along dimension 0, may hold values from -4 to 4
- expert_ids: int32 [2048, 8], P(('grp', 'ep')), parts along dimension 0, may hold values from 0 to 19, as said below
- gate_up: bfloat16 [16, 2048, 1536], P('ep'), may hold values from -0.125 to 0.125
- down: bfloat16 [16, 768, 2048], P('ep'), may hold values from -0.21875 to 0.21875
- hot_gate_up: bfloat16 [16, 2048, 384], P('ep'), may hold values from -0.125 to 0.125
- hot_down: bfloat16 [16, 192, 2048], P('ep'), may hold values from -0.21875 to 0.21875
- helper_list: int32 [16], replicated, may hold values from 0 to 15, as said below
Outputs:
- mixed: bfloat16 [2048, 2048], P(('grp', 'ep')), parts along dimension 0
The draws below stay inside these ranges and needn't reach their ends.
There are 2 independent parts, one for each index of `grp`. The reference program is written for one: setup_inputs(seed, part) draws one part's arguments, and reference() takes and returns one part's arrays. A program takes and returns all parts, laid end to end along the dimension named above; an argument that names none is the same for every part. Nothing has to cross between parts.
Inputs may be any that keep to these rules, and one draw needn't show every extreme that they name: `expert_ids`: each row names 8 different experts; among the 64 tokens of one device every split expert is named by exactly 38 tokens and no owned expert by more than 38. `helper_list`: each device index appears once; the 4 devices of one split expert are an aligned block of 4 consecutive indices.
All inputs are finite; a program needn't handle non-finite values.
Results may differ from the reference program's by a relative error of at most 0.0058.
Values may be sent and summed in bfloat16 or wider, within the bound.
A program may use at most 128 MiB of HBM per device.

```python
import jax
import jax.numpy as jnp
from jax import lax

D = 2048
FF = 768
TOPK = 8
HELP = 4
TOK_DEV = 64
FFH = 192
CAP = 38
TOKENS = 1024
N_EP = 16


def draw_expert_ids(key, part):
    key = jax.random.fold_in(key, 7)
    key_full, key_blocks = jax.random.split(key)
    full_expert = jax.random.randint(key_full, (), 0, N_EP).astype(jnp.int32)
    block_keys = jax.random.split(key_blocks, N_EP)
    split_count = N_EP // HELP
    slot_count = TOK_DEV * TOPK
    hot_total = split_count * CAP
    rest_slots = slot_count - hot_total
    spread_slots = rest_slots - 2 * CAP
    run_length = max(1, -(-spread_slots // (N_EP - 2)))

    def one_block(block_key):
        key_split, key_owned, key_rows, key_cols = jax.random.split(block_key, 4)
        split_order = jax.random.permutation(key_split, split_count).astype(jnp.int32)
        others = (full_expert + 1 + jax.random.permutation(key_owned, N_EP - 1).astype(jnp.int32)) % N_EP
        owned_order = jnp.concatenate([full_expert[None], others]).astype(jnp.int32)
        slot_numbers = jnp.arange(slot_count, dtype=jnp.int32)
        hot_slots = slot_numbers < hot_total
        split_ids = N_EP + split_order[jnp.minimum(slot_numbers // CAP, split_count - 1)]
        offset = slot_numbers - hot_total
        run_index = jnp.where(offset < 2 * CAP, offset // CAP, 2 + (offset - 2 * CAP) // run_length)
        owned_ids = owned_order[jnp.clip(run_index, 0, N_EP - 1)]
        chosen_ids = jnp.where(hot_slots, split_ids, owned_ids)
        id_table = chosen_ids.reshape(TOPK, TOK_DEV).T
        row_order = jax.random.permutation(key_rows, TOK_DEV)
        id_table = id_table[row_order]
        col_shift = jax.random.randint(key_cols, (TOK_DEV, 1), 0, TOPK)
        columns = (jnp.arange(TOPK, dtype=jnp.int32)[None, :] + col_shift) % TOPK
        return jnp.take_along_axis(id_table, columns, axis=1).astype(jnp.int32)
    return jax.vmap(one_block)(block_keys).reshape(N_EP * TOK_DEV, TOPK).astype(jnp.int32)


def draw_helper_list(key, part):
    key = jax.random.fold_in(key, 11)
    key_blocks, key_inside = jax.random.split(key)
    split_count = N_EP // HELP
    block_order = jax.random.permutation(key_blocks, split_count).astype(jnp.int32)
    inside_keys = jax.random.split(key_inside, split_count)
    inside_order = jax.vmap(lambda inner_key: jax.random.permutation(inner_key, HELP))(inside_keys).astype(jnp.int32)
    return (block_order[:, None] * HELP + inside_order).reshape(N_EP).astype(jnp.int32)


def block_scale(key, dims, cuts, least, largest):
    factor_of = 1.0
    for axis_at, blocks in cuts:
        heights = jax.random.uniform(jax.random.fold_in(jax.random.fold_in(key, 6), axis_at), (blocks,), jnp.float32, least / len(cuts), largest / len(cuts))
        factor_of = factor_of * jnp.repeat(jnp.exp(heights), dims[axis_at] // blocks).reshape((-1,) + (1,) * (len(dims) - 1 - axis_at))
    return factor_of


def bell_draw(stream_key, extent, scale, limit, cuts=(), kind=jnp.bfloat16):
    factor_of = block_scale(stream_key, extent, cuts, -0.22, 0.18) if cuts else 1.0
    array = jax.random.normal(stream_key, extent, jnp.float32) * scale * factor_of
    return jnp.minimum(jnp.maximum(array, -limit), limit).astype(kind)


def setup_inputs(seed: int = 0, part: int = 0) -> dict:
    splits = jax.random.split(jax.random.key(seed), 9)
    part_splits = jax.random.split(jax.random.fold_in(splits[8], part), 9)
    return {
        "tokens": bell_draw(part_splits[0], (TOKENS, D), 1.0, 6.0, ((0, 16),)),
        "router_logits": bell_draw(part_splits[1], (TOKENS, TOPK), 1.0, 4.0, ((0, 16),), jnp.float32),
        "expert_ids": draw_expert_ids(jax.random.fold_in(jax.random.fold_in(splits[8], part), 71), part),
        "gate_up": bell_draw(splits[3], (N_EP, D, 2 * FF), D ** -0.5, 0.125, ((0, 16),)),
        "down": bell_draw(splits[4], (N_EP, FF, D), FF ** -0.5, 0.21875, ((0, 16),)),
        "hot_gate_up": bell_draw(splits[5], (N_EP, D, 2 * FFH), D ** -0.5, 0.125, ((0, 16),)),
        "hot_down": bell_draw(splits[6], (N_EP, FFH, D), FF ** -0.5, 0.21875, ((0, 16),)),
        "helper_list": draw_helper_list(jax.random.fold_in(splits[8], 71), part),
    }


def expert_partial(token_rows, gate_up_w, down_w):
    hidden_width = down_w.shape[0]
    projected = jnp.dot(token_rows, gate_up_w, preferred_element_type=jnp.float32)
    hidden = (jax.nn.silu(projected[:, :hidden_width]) * projected[:, hidden_width:]).astype(jnp.bfloat16)
    return jnp.dot(hidden, down_w, preferred_element_type=jnp.float32).astype(jnp.bfloat16)


def routed_rows(expert_ids, shares, expert, capacity):
    matches = expert_ids == expert
    factor_all = jnp.sum(jnp.where(matches, shares, jnp.float32(0.0)), axis=1)
    present = jnp.any(matches, axis=1)
    picked = jnp.nonzero(present, size=capacity, fill_value=0)[0].astype(jnp.int32)
    filled = jnp.sum(present.astype(jnp.int32))
    valid = jnp.arange(capacity, dtype=jnp.int32) < filled
    factor = jnp.where(valid, factor_all[picked], jnp.float32(0.0))
    return picked, factor


def reference(tokens, router_logits, expert_ids, gate_up, down, hot_gate_up, hot_down, helper_list):
    raised = jnp.exp(router_logits)
    shares = raised / jnp.sum(raised, axis=1, keepdims=True)
    capacity = N_EP * CAP
    split_count = N_EP // HELP
    holders = helper_list.reshape(split_count, HELP)

    def regular(running, inputs):
        expert, gate_up_w, down_w = inputs
        picked, factor = routed_rows(expert_ids, shares, expert, capacity)
        partial_value = expert_partial(tokens[picked], gate_up_w, down_w)
        return running.at[picked].add(factor[:, None] * partial_value.astype(jnp.float32)), None

    def split(running, inputs):
        expert, holder_row = inputs
        picked, factor = routed_rows(expert_ids, shares, expert, capacity)
        token_rows = tokens[picked]
        for helper in range(HELP):
            holder = holder_row[helper]
            partial_value = expert_partial(token_rows, hot_gate_up[holder], hot_down[holder])
            running = running.at[picked].add(factor[:, None] * partial_value.astype(jnp.float32))
        return running, None

    running = jnp.zeros((TOKENS, D), jnp.float32)
    running, ignored = lax.scan(regular, running, (jnp.arange(N_EP, dtype=jnp.int32), gate_up, down))
    running, ignored = lax.scan(split, running, (N_EP + jnp.arange(split_count, dtype=jnp.int32), holders))
    return running.astype(jnp.bfloat16)
```

```python
import jax
import jax.numpy as jnp
from jax import lax
from jax.sharding import PartitionSpec as P

HELP = 4


def per_device(
    tokens, router_logits, expert_ids, gate_up, down, hot_gate_up, hot_down, helper_list
):
    devices = lax.axis_size("ep")
    me = lax.axis_index("ep")
    experts = devices + devices // HELP
    raised = jnp.exp(router_logits)
    shares = raised / jnp.sum(raised, axis=1, keepdims=True)
    matches = expert_ids[:, :, None] == jnp.arange(experts, dtype=jnp.int32)[None, None, :]
    table = jnp.sum(jnp.where(matches, shares[:, :, None], jnp.float32(0.0)), axis=1)
    high = table.astype(jnp.bfloat16)
    low = (table - high.astype(jnp.float32)).astype(jnp.bfloat16)
    width = -(-2 * experts // 128) * 128
    extra = jnp.pad(jnp.concatenate([high, low], axis=1), ((0, 0), (0, width - 2 * experts)))
    sent = jnp.concatenate([tokens, extra], axis=1)
    rows = lax.all_gather(sent, "ep", axis=0, tiled=True)
    feature = tokens.shape[1]
    everyone = rows[:, :feature]
    tail = rows[:, feature:]
    split = devices + jnp.sum(
        jnp.where(helper_list == me, jnp.arange(devices, dtype=jnp.int32), 0)
    ) // HELP
    column = jnp.arange(width, dtype=jnp.int32)

    def factor(expert):
        chosen = (column == expert) | (column == expert + experts)
        return jnp.sum(
            jnp.where(chosen[None, :], tail.astype(jnp.float32), 0.0), axis=1, keepdims=True
        )

    def hidden(weights, share):
        projected = jnp.dot(everyone, weights, preferred_element_type=jnp.float32)
        half = weights.shape[1] // 2
        return (jax.nn.silu(projected[:, :half]) * projected[:, half:] * share).astype(
            jnp.bfloat16
        )

    partial = jnp.dot(hidden(gate_up[0], factor(me)), down[0], preferred_element_type=jnp.float32)
    partial = partial + jnp.dot(
        hidden(hot_gate_up[0], factor(split)), hot_down[0], preferred_element_type=jnp.float32
    )
    return lax.psum_scatter(
        partial.astype(jnp.bfloat16), "ep", scatter_dimension=0, tiled=True
    )


def solution(mesh):
    return jax.shard_map(
        per_device,
        mesh=mesh,
        in_specs=(
            P(("grp", "ep"), None),
            P(("grp", "ep"), None),
            P(("grp", "ep"), None),
            P("ep", None, None),
            P("ep", None, None),
            P("ep", None, None),
            P("ep", None, None),
            P(),
        ),
        out_specs=P(("grp", "ep"), None),
        check_vma=False,
    )
```

```python
import functools

import jax
import jax.numpy as jnp
from jax import lax
from jax.experimental import pallas as pl
from jax.experimental.pallas import tpu as pltpu
from jax.sharding import PartitionSpec as P

HELP = 4
MESH = pl.DeviceIdType.MESH


def moe_kernel(
    devices,
    tokens_ref,
    logits_ref,
    ids_ref,
    helper_ref,
    gate_up_hbm,
    down_hbm,
    hot_gate_up_hbm,
    hot_down_hbm,
    out_ref,
    mine,
    rows_ref,
    core_in,
    side_in,
    rail_in,
    total,
    hidden_ref,
    gate_up_ref,
    hot_gate_up_ref,
    down_ref,
    weight_sem,
    send_sem,
    recv_sem,
):
    rails = devices // HELP
    count, feature = tokens_ref.shape
    width = mine.shape[1] - feature
    half = width // 2
    own_width = down_hbm.shape[1]
    hot_width = hot_down_hbm.shape[1]
    me = lax.axis_index("ep")
    rail = me // 4
    side = (me // 2) % 2
    core = me % 2

    def device(r, s, c):
        return {"ep": r * 4 + s * 2 + c}

    def plane(step):
        return lax.rem(rail + step, rails)

    core_peer = device(rail, side, 1 - core)
    side_peer = device(rail, 1 - side, core)
    kept = pl.multiple_of(core * (2 * count), 2 * count)
    given = pl.multiple_of((1 - core) * (2 * count), 2 * count)
    here = pl.multiple_of(core * (2 * count) + side * count, count)
    across = pl.multiple_of(core * (2 * count) + (1 - side) * count, count)
    whole = pl.ds(0, feature)

    def remote(src, dst, kind, step, target):
        return pltpu.make_async_remote_copy(
            src_ref=src,
            dst_ref=dst,
            send_sem=send_sem.at[kind, step],
            recv_sem=recv_sem.at[kind, step],
            device_id=target,
            device_id_type=MESH,
        )

    def gather_rail(step):
        return remote(
            mine,
            rows_ref.at[rail, pl.ds(here, count)],
            0,
            step,
            device(lax.rem(rail - step + rails, rails), side, core),
        )

    def gather_side(step):
        part = rows_ref.at[plane(step), pl.ds(here, count)]
        return remote(part, part, 1, step, side_peer)

    def gather_core(step):
        part = rows_ref.at[plane(step), pl.ds(kept, 2 * count)]
        return remote(part, part, 2, step, core_peer)

    def reduce_core(step):
        return remote(
            rows_ref.at[plane(step), pl.ds(given, 2 * count), whole],
            core_in.at[step],
            3,
            step,
            core_peer,
        )

    def reduce_side(step):
        return remote(
            rows_ref.at[plane(step), pl.ds(across, count), whole],
            side_in.at[step],
            4,
            step,
            side_peer,
        )

    def reduce_rail(step):
        return remote(
            rows_ref.at[plane(step), pl.ds(here, count), whole],
            rail_in.at[step],
            5,
            step,
            device(plane(step), side, core),
        )

    loads = [
        pltpu.make_async_copy(gate_up_hbm.at[0], gate_up_ref, weight_sem.at[0]),
        pltpu.make_async_copy(hot_gate_up_hbm.at[0], hot_gate_up_ref, weight_sem.at[1]),
        pltpu.make_async_copy(
            down_hbm.at[0], down_ref.at[pl.ds(0, own_width)], weight_sem.at[2]
        ),
        pltpu.make_async_copy(
            hot_down_hbm.at[0], down_ref.at[pl.ds(own_width, hot_width)], weight_sem.at[3]
        ),
    ]
    for load in loads:
        load.start()

    barrier = pltpu.get_barrier_semaphore()
    pl.semaphore_signal(barrier, inc=1, device_id=core_peer, device_id_type=MESH)
    pl.semaphore_signal(barrier, inc=1, device_id=side_peer, device_id_type=MESH)
    for step in range(1, rails):
        pl.semaphore_signal(
            barrier, inc=1, device_id=device(plane(step), side, core), device_id_type=MESH
        )

    raised = jnp.exp(logits_ref[...])
    shares = raised / jnp.sum(raised, axis=1, keepdims=True)
    chosen = ids_ref[...]
    column = lax.broadcasted_iota(jnp.int32, (count, width), 1)
    expert = jnp.where(column < half, column, column - half)
    table = jnp.zeros((count, width), jnp.float32)
    for k in range(chosen.shape[1]):
        table = table + jnp.where(expert == chosen[:, k : k + 1], shares[:, k : k + 1], 0.0)
    high = table.astype(jnp.bfloat16).astype(jnp.float32)
    table = jnp.where(column < half, high, table - high).astype(jnp.bfloat16)
    held = tokens_ref[...]
    mine[:, pl.ds(0, feature)] = held
    mine[:, pl.ds(feature, width)] = table
    rows_ref[rail, pl.ds(here, count), pl.ds(0, feature)] = held
    rows_ref[rail, pl.ds(here, count), pl.ds(feature, width)] = table

    helper = helper_ref[...]
    entry = lax.broadcasted_iota(jnp.int32, helper.shape, 1)
    position = jnp.sum(jnp.where(helper == me, entry, 0), axis=1, keepdims=True)
    split = devices + position // HELP

    pl.semaphore_wait(barrier, rails + 1)
    gather_side(0).start()
    for step in range(1, rails):
        gather_rail(step).start()

    def to_side(step):
        reduce_core(step).wait_recv()
        at = plane(step)
        theirs = pl.ds(pl.multiple_of((1 - side) * count, count), count)
        rows_ref[at, pl.ds(across, count), whole] = (
            rows_ref[at, pl.ds(across, count), whole].astype(jnp.float32)
            + core_in[step, theirs, :].astype(jnp.float32)
        ).astype(jnp.bfloat16)
        reduce_side(step).start()

    def plane_sum(step):
        reduce_side(step).wait_recv()
        ours = pl.ds(pl.multiple_of(side * count, count), count)
        return (
            rows_ref[plane(step), pl.ds(here, count), whole].astype(jnp.float32)
            + core_in[step, ours, :].astype(jnp.float32)
            + side_in[step].astype(jnp.float32)
        )

    def to_rail(step):
        rows_ref[plane(step), pl.ds(here, count), whole] = plane_sum(step).astype(jnp.bfloat16)
        reduce_rail(step).start()

    def stage(step, carry):
        at = plane(step)

        @pl.when(step + 1 < rails)
        def _():
            gather_rail(step + 1).wait_recv()
            gather_side(step + 1).start()

        gather_side(step).wait_recv()
        gather_core(step).start()

        @pl.when(step == 0)
        def _():
            for load in loads[:2]:
                load.wait()

        gather_core(step).wait_recv()
        tokens = rows_ref[at, :, pl.ds(0, feature)]
        tail = rows_ref[at, :, pl.ds(feature, width)].astype(jnp.float32)
        lane = lax.broadcasted_iota(jnp.int32, (1, width), 1)
        lane = jnp.where(lane < half, lane, lane - half)
        own_share = jnp.sum(jnp.where(lane == me, tail, 0.0), axis=1, keepdims=True)
        hot_share = jnp.sum(jnp.where(lane == split, tail, 0.0), axis=1, keepdims=True)
        tile = 256
        for at_column in range(0, own_width, tile):
            gate = jnp.dot(
                tokens,
                gate_up_ref[:, pl.ds(at_column, tile)],
                preferred_element_type=jnp.float32,
            )
            up = jnp.dot(
                tokens,
                gate_up_ref[:, pl.ds(own_width + at_column, tile)],
                preferred_element_type=jnp.float32,
            )
            hidden_ref[:, pl.ds(at_column, tile)] = (
                jax.nn.silu(gate) * up * own_share
            ).astype(jnp.bfloat16)
        both = jnp.dot(tokens, hot_gate_up_ref[...], preferred_element_type=jnp.float32)
        hidden_ref[:, pl.ds(own_width, hot_width)] = (
            jax.nn.silu(both[:, :hot_width]) * both[:, hot_width:] * hot_share
        ).astype(jnp.bfloat16)

        @pl.when(step >= 1)
        def _():
            to_side(step - 1)

        @pl.when(step >= 3)
        def _():
            to_rail(step - 2)

        @pl.when(step == 2)
        def _():
            total[...] = plane_sum(0)

        @pl.when(step == 0)
        def _():
            for load in loads[2:]:
                load.wait()

        gather_side(step).wait_send()
        gather_core(step).wait_send()
        hidden = hidden_ref[...]
        for at_column in range(0, feature, 512):
            rows_ref[at, :, pl.ds(at_column, 512)] = jnp.dot(
                hidden,
                down_ref[:, pl.ds(at_column, 512)],
                preferred_element_type=jnp.float32,
            ).astype(jnp.bfloat16)
        reduce_core(step).start()
        return carry

    lax.fori_loop(0, rails, stage, 0)
    to_side(rails - 1)
    to_rail(rails - 2)
    to_rail(rails - 1)
    result = total[...]
    for step in range(1, rails):
        reduce_rail(step).wait_recv()
        result = result + rail_in[step].astype(jnp.float32)
    out_ref[...] = result.astype(jnp.bfloat16)
    for step in range(rails):
        reduce_core(step).wait_send()
        reduce_side(step).wait_send()
        if step:
            gather_rail(step).wait_send()
            reduce_rail(step).wait_send()


def per_device(
    tokens, router_logits, expert_ids, gate_up, down, hot_gate_up, hot_down, helper_list
):
    devices = lax.axis_size("ep")
    rails = devices // HELP
    count, feature = tokens.shape
    experts = devices + rails
    half = -(-experts // 64) * 64
    width = 2 * half
    hidden = down.shape[1] + hot_down.shape[1]
    bf16 = jnp.bfloat16
    vmem = pl.BlockSpec(memory_space=pltpu.VMEM)
    hbm = pl.BlockSpec(memory_space=pl.ANY)
    return pl.pallas_call(
        functools.partial(moe_kernel, devices),
        out_shape=jax.ShapeDtypeStruct((count, feature), bf16),
        in_specs=[vmem] * 4 + [hbm] * 4,
        out_specs=vmem,
        scratch_shapes=[
            pltpu.VMEM((count, feature + width), bf16),
            pltpu.VMEM((rails, HELP * count, feature + width), bf16),
            pltpu.VMEM((rails, 2 * count, feature), bf16),
            pltpu.VMEM((rails, count, feature), bf16),
            pltpu.VMEM((rails, count, feature), bf16),
            pltpu.VMEM((count, feature), jnp.float32),
            pltpu.VMEM((HELP * count, hidden), bf16),
            pltpu.VMEM(gate_up.shape[1:], bf16),
            pltpu.VMEM(hot_gate_up.shape[1:], bf16),
            pltpu.VMEM((hidden, feature), bf16),
            pltpu.SemaphoreType.DMA((4,)),
            pltpu.SemaphoreType.DMA((6, rails)),
            pltpu.SemaphoreType.DMA((6, rails)),
        ],
        compiler_params=pltpu.CompilerParams(
            collective_id=0, has_side_effects=True, vmem_limit_bytes=60 * 1024 * 1024
        ),
    )(
        tokens,
        router_logits,
        expert_ids,
        helper_list.reshape(1, devices),
        gate_up,
        down,
        hot_gate_up,
        hot_down,
    )


def solution(mesh):
    return jax.shard_map(
        per_device,
        mesh=mesh,
        in_specs=(
            P(("grp", "ep"), None),
            P(("grp", "ep"), None),
            P(("grp", "ep"), None),
            P("ep", None, None),
            P("ep", None, None),
            P("ep", None, None),
            P("ep", None, None),
            P(),
        ),
        out_specs=P(("grp", "ep"), None),
        check_vma=False,
    )
```

```python
import functools

import jax
import jax.numpy as jnp
from jax import lax
from jax.experimental import pallas as pl
from jax.experimental.pallas import tpu as pltpu
from jax.sharding import PartitionSpec as P

HELP = 4
MESH = pl.DeviceIdType.MESH


def moe_kernel(
    devices,
    tokens_ref,
    logits_ref,
    ids_ref,
    helper_ref,
    gate_up_hbm,
    down_hbm,
    hot_gate_up_hbm,
    hot_down_hbm,
    out_ref,
    mine,
    rows_ref,
    core_in,
    side_in,
    rail_in,
    hidden_ref,
    gate_up_ref,
    hot_gate_up_ref,
    down_ref,
    weight_sem,
    send_sem,
    recv_sem,
):
    rails = devices // HELP
    count, feature = tokens_ref.shape
    width = mine.shape[1] - feature
    half = width // 2
    own_width = down_hbm.shape[1]
    hot_width = hot_down_hbm.shape[1]
    me = lax.axis_index("ep")
    rail = me // 4
    side = (me // 2) % 2
    core = me % 2

    def device(r, s, c):
        return {"ep": r * 4 + s * 2 + c}

    def plane(step):
        offset = jnp.where(step < 2, step, rails + 1 - step)
        partner = 0
        bit = 1
        while bit < rails:
            partner = partner + bit * ((rail // bit + offset // bit) % 2)
            bit *= 2
        return partner

    core_peer = device(rail, side, 1 - core)
    side_peer = device(rail, 1 - side, core)
    kept = pl.multiple_of(core * (2 * count), 2 * count)
    given = pl.multiple_of((1 - core) * (2 * count), 2 * count)
    here = pl.multiple_of(core * (2 * count) + side * count, count)
    across = pl.multiple_of(core * (2 * count) + (1 - side) * count, count)
    whole = pl.ds(0, feature)

    def remote(src, dst, kind, step, target):
        return pltpu.make_async_remote_copy(
            src_ref=src,
            dst_ref=dst,
            send_sem=send_sem.at[kind, step],
            recv_sem=recv_sem.at[kind, step],
            device_id=target,
            device_id_type=MESH,
        )

    def gather_rail(step):
        return remote(
            mine,
            rows_ref.at[rail, pl.ds(here, count)],
            0,
            step,
            device(plane(step), side, core),
        )

    def gather_side(step):
        part = rows_ref.at[plane(step), pl.ds(here, count)]
        return remote(part, part, 1, step, side_peer)

    def gather_core(step):
        part = rows_ref.at[plane(step), pl.ds(kept, 2 * count)]
        return remote(part, part, 2, step, core_peer)

    def reduce_core(step):
        return remote(
            rows_ref.at[plane(step), pl.ds(given, 2 * count), whole],
            core_in.at[step],
            3,
            step,
            core_peer,
        )

    def reduce_side(step):
        return remote(
            rows_ref.at[plane(step), pl.ds(across, count), whole],
            side_in.at[step],
            4,
            step,
            side_peer,
        )

    def reduce_rail(step):
        return remote(
            rows_ref.at[plane(step), pl.ds(here, count), whole],
            rail_in.at[step],
            5,
            step,
            device(plane(step), side, core),
        )

    loads = [
        pltpu.make_async_copy(gate_up_hbm.at[0], gate_up_ref, weight_sem.at[0]),
        pltpu.make_async_copy(hot_gate_up_hbm.at[0], hot_gate_up_ref, weight_sem.at[1]),
        pltpu.make_async_copy(
            down_hbm.at[0], down_ref.at[pl.ds(0, own_width)], weight_sem.at[2]
        ),
        pltpu.make_async_copy(
            hot_down_hbm.at[0], down_ref.at[pl.ds(own_width, hot_width)], weight_sem.at[3]
        ),
    ]
    for load in loads:
        load.start()

    barrier = pltpu.get_barrier_semaphore()
    pl.semaphore_signal(barrier, inc=1, device_id=core_peer, device_id_type=MESH)
    pl.semaphore_signal(barrier, inc=1, device_id=side_peer, device_id_type=MESH)
    for step in range(1, rails):
        pl.semaphore_signal(
            barrier, inc=1, device_id=device(plane(step), side, core), device_id_type=MESH
        )

    raised = jnp.exp(logits_ref[...])
    shares = raised / jnp.sum(raised, axis=1, keepdims=True)
    chosen = ids_ref[...]
    column = lax.broadcasted_iota(jnp.int32, (count, width), 1)
    expert = jnp.where(column < half, column, column - half)
    table = jnp.zeros((count, width), jnp.float32)
    for k in range(chosen.shape[1]):
        table = table + jnp.where(expert == chosen[:, k : k + 1], shares[:, k : k + 1], 0.0)
    high = table.astype(jnp.bfloat16).astype(jnp.float32)
    table = jnp.where(column < half, high, table - high).astype(jnp.bfloat16)
    held = tokens_ref[...]
    mine[:, pl.ds(0, feature)] = held
    mine[:, pl.ds(feature, width)] = table
    rows_ref[rail, pl.ds(here, count), pl.ds(0, feature)] = held
    rows_ref[rail, pl.ds(here, count), pl.ds(feature, width)] = table

    helper = helper_ref[...]
    entry = lax.broadcasted_iota(jnp.int32, helper.shape, 1)
    position = jnp.sum(jnp.where(helper == me, entry, 0), axis=1, keepdims=True)
    split = devices + position // HELP

    pl.semaphore_wait(barrier, rails + 1)
    gather_side(0).start()
    gather_rail(1).start()
    gather_rail(2).start()

    def to_side(step):
        reduce_core(step).wait_recv()
        at = plane(step)
        theirs = pl.ds(pl.multiple_of((1 - side) * count, count), count)
        rows_ref[at, pl.ds(across, count), whole] = (
            rows_ref[at, pl.ds(across, count), whole].astype(jnp.float32)
            + core_in[step, theirs, :].astype(jnp.float32)
        ).astype(jnp.bfloat16)
        reduce_side(step).start()

    def plane_sum(step):
        reduce_side(step).wait_recv()
        ours = pl.ds(pl.multiple_of(side * count, count), count)
        return (
            rows_ref[plane(step), pl.ds(here, count), whole].astype(jnp.float32)
            + core_in[step, ours, :].astype(jnp.float32)
            + side_in[step].astype(jnp.float32)
        )

    def to_rail(step):
        rows_ref[plane(step), pl.ds(here, count), whole] = plane_sum(step).astype(jnp.bfloat16)
        reduce_rail(step).start()

    gather_rail(1).wait_recv()
    gather_side(1).start()
    gather_side(0).wait_recv()
    gather_core(0).start()

    def stage(index, carry):
        step = lax.rem(index + 1, rails)
        at = plane(step)

        def next_rail():
            gather_rail(index + 2).wait_recv()
            gather_side(index + 2).start()

            @pl.when(index + 3 < rails)
            def _():
                gather_rail(index + 3).start()

        pl.when(index + 3 < rails)(next_rail)

        @pl.when(step > 0)
        def _():
            gather_side(step).wait_recv()
            gather_core(step).start()

        @pl.when(index == 0)
        def _():
            for load in loads[:2]:
                load.wait()

        gather_core(step).wait_recv()
        tokens = rows_ref[at, :, pl.ds(0, feature)]
        tail = rows_ref[at, :, pl.ds(feature, width)].astype(jnp.float32)
        lane = lax.broadcasted_iota(jnp.int32, (1, width), 1)
        lane = jnp.where(lane < half, lane, lane - half)
        own_share = jnp.sum(jnp.where(lane == me, tail, 0.0), axis=1, keepdims=True)
        hot_share = jnp.sum(jnp.where(lane == split, tail, 0.0), axis=1, keepdims=True)
        tile = 256
        for at_column in range(0, own_width, tile):
            gate = jnp.dot(
                tokens,
                gate_up_ref[:, pl.ds(at_column, tile)],
                preferred_element_type=jnp.float32,
            )
            up = jnp.dot(
                tokens,
                gate_up_ref[:, pl.ds(own_width + at_column, tile)],
                preferred_element_type=jnp.float32,
            )
            hidden_ref[:, pl.ds(at_column, tile)] = (
                jax.nn.silu(gate) * up * own_share
            ).astype(jnp.bfloat16)
        both = jnp.dot(tokens, hot_gate_up_ref[...], preferred_element_type=jnp.float32)
        hidden_ref[:, pl.ds(own_width, hot_width)] = (
            jax.nn.silu(both[:, :hot_width]) * both[:, hot_width:] * hot_share
        ).astype(jnp.bfloat16)

        pl.when(index + 3 == rails)(next_rail)

        @pl.when(index >= 1)
        def _():
            to_side(index)

        @pl.when(index >= 2)
        def _():
            to_rail(index - 1)

        @pl.when(index == 0)
        def _():
            for load in loads[2:]:
                load.wait()

        gather_side(step).wait_send()
        gather_core(step).wait_send()
        hidden = hidden_ref[...]
        for at_column in range(0, feature, 512):
            rows_ref[at, :, pl.ds(at_column, 512)] = jnp.dot(
                hidden,
                down_ref[:, pl.ds(at_column, 512)],
                preferred_element_type=jnp.float32,
            ).astype(jnp.bfloat16)
        reduce_core(step).start()
        return carry

    lax.fori_loop(0, rails, stage, 0)
    to_rail(rails - 1)
    to_side(0)
    result = plane_sum(0)
    for step in range(1, rails):
        reduce_rail(step).wait_recv()
        result = result + rail_in[step].astype(jnp.float32)
    out_ref[...] = result.astype(jnp.bfloat16)
    for step in range(rails):
        reduce_core(step).wait_send()
        reduce_side(step).wait_send()
        if step:
            gather_rail(step).wait_send()
            reduce_rail(step).wait_send()


def per_device(
    tokens, router_logits, expert_ids, gate_up, down, hot_gate_up, hot_down, helper_list
):
    devices = lax.axis_size("ep")
    rails = devices // HELP
    count, feature = tokens.shape
    experts = devices + rails
    half = -(-experts // 64) * 64
    width = 2 * half
    hidden = down.shape[1] + hot_down.shape[1]
    bf16 = jnp.bfloat16
    vmem = pl.BlockSpec(memory_space=pltpu.VMEM)
    hbm = pl.BlockSpec(memory_space=pl.ANY)
    return pl.pallas_call(
        functools.partial(moe_kernel, devices),
        out_shape=jax.ShapeDtypeStruct((count, feature), bf16),
        in_specs=[vmem] * 4 + [hbm] * 4,
        out_specs=vmem,
        scratch_shapes=[
            pltpu.VMEM((count, feature + width), bf16),
            pltpu.VMEM((rails, HELP * count, feature + width), bf16),
            pltpu.VMEM((rails, 2 * count, feature), bf16),
            pltpu.VMEM((rails, count, feature), bf16),
            pltpu.VMEM((rails, count, feature), bf16),
            pltpu.VMEM((HELP * count, hidden), bf16),
            pltpu.VMEM(gate_up.shape[1:], bf16),
            pltpu.VMEM(hot_gate_up.shape[1:], bf16),
            pltpu.VMEM((hidden, feature), bf16),
            pltpu.SemaphoreType.DMA((4,)),
            pltpu.SemaphoreType.DMA((6, rails)),
            pltpu.SemaphoreType.DMA((6, rails)),
        ],
        compiler_params=pltpu.CompilerParams(
            collective_id=0, has_side_effects=True, vmem_limit_bytes=60 * 1024 * 1024
        ),
    )(
        tokens,
        router_logits,
        expert_ids,
        helper_list.reshape(1, devices),
        gate_up,
        down,
        hot_gate_up,
        hot_down,
    )


def solution(mesh):
    return jax.shard_map(
        per_device,
        mesh=mesh,
        in_specs=(
            P(("grp", "ep"), None),
            P(("grp", "ep"), None),
            P(("grp", "ep"), None),
            P("ep", None, None),
            P("ep", None, None),
            P("ep", None, None),
            P("ep", None, None),
            P(),
        ),
        out_specs=P(("grp", "ep"), None),
        check_vma=False,
    )
```

```python
import functools

import jax
import jax.numpy as jnp
from jax import lax
from jax.experimental import pallas as pl
from jax.experimental.pallas import tpu as pltpu
from jax.sharding import PartitionSpec as P

HELP = 4
MESH = pl.DeviceIdType.MESH


def moe_kernel(
    devices,
    tokens_ref,
    logits_ref,
    ids_ref,
    helper_ref,
    gate_up_hbm,
    down_hbm,
    hot_gate_up_hbm,
    hot_down_hbm,
    out_ref,
    mine,
    rows_ref,
    core_in,
    side_in,
    rail_in,
    hidden_ref,
    gate_up_ref,
    hot_gate_up_ref,
    down_ref,
    weight_sem,
    send_sem,
    recv_sem,
):
    rails = devices // HELP
    count, feature = tokens_ref.shape
    width = mine.shape[1] - feature
    half = width // 2
    own_width = down_hbm.shape[1]
    hot_width = hot_down_hbm.shape[1]
    me = lax.axis_index("ep")
    rail = me // 4
    side = (me // 2) % 2
    core = me % 2

    def device(r, s, c):
        return {"ep": r * 4 + s * 2 + c}

    def plane(step):
        offset = jnp.where(step < 2, step, rails + 1 - step)
        partner = 0
        bit = 1
        while bit < rails:
            partner = partner + bit * ((rail // bit + offset // bit) % 2)
            bit *= 2
        return partner

    core_peer = device(rail, side, 1 - core)
    side_peer = device(rail, 1 - side, core)
    kept = pl.multiple_of(core * (2 * count), 2 * count)
    given = pl.multiple_of((1 - core) * (2 * count), 2 * count)
    here = pl.multiple_of(core * (2 * count) + side * count, count)
    across = pl.multiple_of(core * (2 * count) + (1 - side) * count, count)
    whole = pl.ds(0, feature)

    def remote(src, dst, kind, step, target):
        return pltpu.make_async_remote_copy(
            src_ref=src,
            dst_ref=dst,
            send_sem=send_sem.at[kind, step],
            recv_sem=recv_sem.at[kind, step],
            device_id=target,
            device_id_type=MESH,
        )

    def gather_rail(step):
        return remote(
            mine,
            rows_ref.at[rail, pl.ds(here, count)],
            0,
            step,
            device(plane(step), side, core),
        )

    def gather_side(step):
        part = rows_ref.at[plane(step), pl.ds(here, count)]
        return remote(part, part, 1, step, side_peer)

    def gather_core(step):
        part = rows_ref.at[plane(step), pl.ds(kept, 2 * count)]
        return remote(part, part, 2, step, core_peer)

    def reduce_core(step):
        return remote(
            rows_ref.at[plane(step), pl.ds(given, 2 * count), whole],
            core_in.at[step],
            3,
            step,
            core_peer,
        )

    def reduce_side(step):
        return remote(
            rows_ref.at[plane(step), pl.ds(across, count), whole],
            side_in.at[step],
            4,
            step,
            side_peer,
        )

    def reduce_rail(step):
        return remote(
            rows_ref.at[plane(step), pl.ds(here, count), whole],
            rail_in.at[step],
            5,
            step,
            device(plane(step), side, core),
        )

    loads = [
        pltpu.make_async_copy(gate_up_hbm.at[0], gate_up_ref, weight_sem.at[0]),
        pltpu.make_async_copy(hot_gate_up_hbm.at[0], hot_gate_up_ref, weight_sem.at[1]),
        pltpu.make_async_copy(
            down_hbm.at[0], down_ref.at[pl.ds(0, own_width)], weight_sem.at[2]
        ),
        pltpu.make_async_copy(
            hot_down_hbm.at[0], down_ref.at[pl.ds(own_width, hot_width)], weight_sem.at[3]
        ),
    ]
    for load in loads:
        load.start()

    barrier = pltpu.get_barrier_semaphore()
    pl.semaphore_signal(barrier, inc=1, device_id=core_peer, device_id_type=MESH)
    pl.semaphore_signal(barrier, inc=1, device_id=side_peer, device_id_type=MESH)
    for step in range(1, rails):
        pl.semaphore_signal(
            barrier, inc=1, device_id=device(plane(step), side, core), device_id_type=MESH
        )

    raised = jnp.exp(logits_ref[...])
    shares = raised / jnp.sum(raised, axis=1, keepdims=True)
    chosen = ids_ref[...]
    column = lax.broadcasted_iota(jnp.int32, (count, width), 1)
    expert = jnp.where(column < half, column, column - half)
    table = jnp.zeros((count, width), jnp.float32)
    for k in range(chosen.shape[1]):
        table = table + jnp.where(expert == chosen[:, k : k + 1], shares[:, k : k + 1], 0.0)
    high = table.astype(jnp.bfloat16).astype(jnp.float32)
    table = jnp.where(column < half, high, table - high).astype(jnp.bfloat16)
    held = tokens_ref[...]
    mine[:, pl.ds(0, feature)] = held
    mine[:, pl.ds(feature, width)] = table
    rows_ref[rail, pl.ds(here, count), pl.ds(0, feature)] = held
    rows_ref[rail, pl.ds(here, count), pl.ds(feature, width)] = table

    helper = helper_ref[...]
    entry = lax.broadcasted_iota(jnp.int32, helper.shape, 1)
    position = jnp.sum(jnp.where(helper == me, entry, 0), axis=1, keepdims=True)
    split = devices + position // HELP

    pl.semaphore_wait(barrier, rails + 1)
    gather_side(0).start()
    gather_rail(1).start()
    gather_rail(2).start()

    def to_side(step):
        reduce_core(step).wait_recv()
        at = plane(step)
        theirs = pl.ds(pl.multiple_of((1 - side) * count, count), count)
        rows_ref[at, pl.ds(across, count), whole] = (
            rows_ref[at, pl.ds(across, count), whole].astype(jnp.float32)
            + core_in[step, theirs, :].astype(jnp.float32)
        ).astype(jnp.bfloat16)
        reduce_side(step).start()

    def plane_sum(step):
        reduce_side(step).wait_recv()
        ours = pl.ds(pl.multiple_of(side * count, count), count)
        return (
            rows_ref[plane(step), pl.ds(here, count), whole].astype(jnp.float32)
            + core_in[step, ours, :].astype(jnp.float32)
            + side_in[step].astype(jnp.float32)
        )

    def to_rail(step):
        rows_ref[plane(step), pl.ds(here, count), whole] = plane_sum(step).astype(jnp.bfloat16)
        reduce_rail(step).start()

    gather_rail(1).wait_recv()
    gather_side(1).start()
    gather_side(0).wait_recv()
    gather_core(0).start()

    def stage(index, carry):
        step = lax.rem(index + 1, rails)
        at = plane(step)

        def next_rail():
            gather_rail(index + 2).wait_recv()
            gather_side(index + 2).start()

            @pl.when(index + 3 < rails)
            def _():
                gather_rail(index + 3).start()

        pl.when(index + 3 < rails)(next_rail)

        @pl.when(step > 0)
        def _():
            gather_side(step).wait_recv()
            gather_core(step).start()

        @pl.when(index >= 1)
        def _():
            to_side(index)

        @pl.when(index == 0)
        def _():
            for load in loads[:2]:
                load.wait()

        gather_core(step).wait_recv()
        tokens = rows_ref[at, :, pl.ds(0, feature)]
        tail = rows_ref[at, :, pl.ds(feature, width)].astype(jnp.float32)
        lane = lax.broadcasted_iota(jnp.int32, (1, width), 1)
        lane = jnp.where(lane < half, lane, lane - half)
        own_share = jnp.sum(jnp.where(lane == me, tail, 0.0), axis=1, keepdims=True)
        hot_share = jnp.sum(jnp.where(lane == split, tail, 0.0), axis=1, keepdims=True)
        tile = 256
        for at_column in range(0, own_width, tile):
            gate = jnp.dot(
                tokens,
                gate_up_ref[:, pl.ds(at_column, tile)],
                preferred_element_type=jnp.float32,
            )
            up = jnp.dot(
                tokens,
                gate_up_ref[:, pl.ds(own_width + at_column, tile)],
                preferred_element_type=jnp.float32,
            )
            hidden_ref[:, pl.ds(at_column, tile)] = (
                jax.nn.silu(gate) * up * own_share
            ).astype(jnp.bfloat16)
        both = jnp.dot(tokens, hot_gate_up_ref[...], preferred_element_type=jnp.float32)
        hidden_ref[:, pl.ds(own_width, hot_width)] = (
            jax.nn.silu(both[:, :hot_width]) * both[:, hot_width:] * hot_share
        ).astype(jnp.bfloat16)

        pl.when(index + 3 == rails)(next_rail)

        @pl.when(index == 0)
        def _():
            for load in loads[2:]:
                load.wait()

        gather_side(step).wait_send()
        gather_core(step).wait_send()
        hidden = hidden_ref[...]
        for at_column in range(0, feature, 512):
            rows_ref[at, :, pl.ds(at_column, 512)] = jnp.dot(
                hidden,
                down_ref[:, pl.ds(at_column, 512)],
                preferred_element_type=jnp.float32,
            ).astype(jnp.bfloat16)
        reduce_core(step).start()

        @pl.when(index >= 1)
        def _():
            to_rail(index)

        return carry

    lax.fori_loop(0, rails, stage, 0)
    to_side(0)
    result = plane_sum(0)
    for step in range(1, rails):
        reduce_rail(step).wait_recv()
        result = result + rail_in[step].astype(jnp.float32)
    out_ref[...] = result.astype(jnp.bfloat16)
    for step in range(rails):
        reduce_core(step).wait_send()
        reduce_side(step).wait_send()
        if step:
            gather_rail(step).wait_send()
            reduce_rail(step).wait_send()


def per_device(
    tokens, router_logits, expert_ids, gate_up, down, hot_gate_up, hot_down, helper_list
):
    devices = lax.axis_size("ep")
    rails = devices // HELP
    count, feature = tokens.shape
    experts = devices + rails
    half = -(-experts // 64) * 64
    width = 2 * half
    hidden = down.shape[1] + hot_down.shape[1]
    bf16 = jnp.bfloat16
    vmem = pl.BlockSpec(memory_space=pltpu.VMEM)
    hbm = pl.BlockSpec(memory_space=pl.ANY)
    return pl.pallas_call(
        functools.partial(moe_kernel, devices),
        out_shape=jax.ShapeDtypeStruct((count, feature), bf16),
        in_specs=[vmem] * 4 + [hbm] * 4,
        out_specs=vmem,
        scratch_shapes=[
            pltpu.VMEM((count, feature + width), bf16),
            pltpu.VMEM((rails, HELP * count, feature + width), bf16),
            pltpu.VMEM((rails, 2 * count, feature), bf16),
            pltpu.VMEM((rails, count, feature), bf16),
            pltpu.VMEM((rails, count, feature), bf16),
            pltpu.VMEM((HELP * count, hidden), bf16),
            pltpu.VMEM(gate_up.shape[1:], bf16),
            pltpu.VMEM(hot_gate_up.shape[1:], bf16),
            pltpu.VMEM((hidden, feature), bf16),
            pltpu.SemaphoreType.DMA((4,)),
            pltpu.SemaphoreType.DMA((6, rails)),
            pltpu.SemaphoreType.DMA((6, rails)),
        ],
        compiler_params=pltpu.CompilerParams(
            collective_id=0, has_side_effects=True, vmem_limit_bytes=60 * 1024 * 1024
        ),
    )(
        tokens,
        router_logits,
        expert_ids,
        helper_list.reshape(1, devices),
        gate_up,
        down,
        hot_gate_up,
        hot_down,
    )


def solution(mesh):
    return jax.shard_map(
        per_device,
        mesh=mesh,
        in_specs=(
            P(("grp", "ep"), None),
            P(("grp", "ep"), None),
            P(("grp", "ep"), None),
            P("ep", None, None),
            P("ep", None, None),
            P("ep", None, None),
            P("ep", None, None),
            P(),
        ),
        out_specs=P(("grp", "ep"), None),
        check_vma=False,
    )
```
